256 devices in a mesh: layer: 16 (over y_lo, x, core), query: 16 (over z, y_hi).
Axes of the slice: x: 4, y: 4 (y_hi: 2, y_lo: 2; y = y_hi * 2 + y_lo), z: 8, core: 2. Of those that a mesh axis runs over, the one named last changes fastest.
Arguments:
- queries: bfloat16 [16384, 16, 4096], P('query', 'layer'), may hold values from -6 to 6
- train_grads: bfloat16 [1024, 16, 4096], P('query', 'layer'), may hold values from -6 to 6
- basis_out: float32 [16, 64, 64], P('layer'), may hold values from -0.75 to 0.75
- basis_in: float32 [16, 64, 64], P('layer'), may hold values from -0.75 to 0.75
- eig_values: float32 [16, 4096], P('layer'), may hold values from 0.1 to 2
- train_order: int32 [1024], replicated, may hold values from 0 to 1023, each once
Outputs:
- scores: float32 [1024, 16384], P('layer', 'query')
The draws below stay inside these ranges and needn't reach their ends.
Inputs may be any that keep to these rules, and one draw needn't show every extreme that they name: `train_order`: a permutation of the 1024 training examples.
All inputs are finite; a program needn't handle non-finite values.
Results may differ from the reference program's by a relative error of at most 0.0029.
Values may be sent and summed in bfloat16 or wider, within the bound.
No kernel may reach another device: no remote copies, remote signals or barrier semaphores. Data moves between devices by JAX's collectives and lax.ppermute only.
A program may use at most 64 MiB of HBM per device.

```python
import math
import jax
import jax.numpy as jnp
from jax import lax

PROJ = 64
FEAT = 4096
LAYERS = 16
QUERIES = 16384
TRAIN = 1024


def block_levels(stream_key, dims, cuts, smallest, top_value):
    def one(axis_at, blocks):
        heights = jax.random.uniform(jax.random.fold_in(jax.random.fold_in(stream_key, 6), axis_at), (blocks,), jnp.float32, smallest / len(cuts), top_value / len(cuts))
        return jnp.repeat(jnp.exp(heights), dims[axis_at] // blocks).reshape((-1,) + (1,) * (len(dims) - axis_at - 1))

    gain = one(*cuts[0])
    for cut in cuts[1:]:
        gain = gain * one(*cut)
    return gain


def gaussian(own_key, shape, width, bound, shards=(), held_as=jnp.bfloat16):
    entries = width * jax.random.normal(own_key, shape, jnp.float32)
    if shards:
        entries = entries * block_levels(own_key, shape, shards, -0.22, 0.18)
    return jnp.clip(entries, -bound, bound).astype(held_as)


def setup_inputs(seed: int = 0) -> dict:
    key_list = jax.random.split(jax.random.key(seed), 7)
    queries = gaussian(key_list[0], (QUERIES, LAYERS, FEAT), 1.0, 6.0, ((0, 16), (1, 16)))
    train_grads = gaussian(key_list[1], (TRAIN, LAYERS, FEAT), 1.0, 6.0, ((0, 16), (1, 16)))
    basis_out = gaussian(key_list[2], (LAYERS, PROJ, PROJ), PROJ ** -0.5, 0.75, ((0, 16),), jnp.float32)
    basis_in = gaussian(key_list[3], (LAYERS, PROJ, PROJ), PROJ ** -0.5, 0.75, ((0, 16),), jnp.float32)
    eig_values = jnp.clip(jnp.exp(math.log(2.0) - 2.9957323 * jax.random.uniform(key_list[4], (LAYERS, FEAT), jnp.float32) ** block_levels(key_list[4], (LAYERS, FEAT), ((0, 16),), -0.2, 0.2)), 0.1, 2.0)
    train_order = jax.random.permutation(key_list[5], TRAIN).astype(jnp.int32)
    return dict(queries=queries, train_grads=train_grads, basis_out=basis_out, basis_in=basis_in, eig_values=eig_values, train_order=train_order)


def reference(queries, train_grads, basis_out, basis_in, eig_values, train_order):
    layer_count = queries.shape[1]
    grads_full = train_grads.astype(jnp.float32).reshape(TRAIN, layer_count, PROJ, PROJ)
    rotated = jnp.einsum('lab,elac,lcd->elbd', basis_out, grads_full, basis_in, precision=lax.Precision.HIGHEST)
    scaled = (rotated.reshape(TRAIN, layer_count, FEAT) / eig_values[None]).astype(jnp.bfloat16)

    def add_layer(layer_index, running):
        train_layer = lax.dynamic_index_in_dim(scaled, layer_index, 1, keepdims=False)
        query_layer = lax.dynamic_index_in_dim(queries, layer_index, 1, keepdims=False)
        partial_sum = lax.dot_general(train_layer, query_layer, (((1,), (1,)), ((), ())), preferred_element_type=jnp.float32)
        return running + partial_sum
    total = lax.fori_loop(0, layer_count, add_layer, jnp.zeros((TRAIN, queries.shape[0]), jnp.float32))
    factor = 1.0 / jnp.sqrt(jnp.float32(layer_count * FEAT))
    return total[train_order.astype(jnp.int32)] * factor
```

```python
import jax
import jax.numpy as jnp
from jax import lax
from jax.sharding import PartitionSpec as P

Z = 8
Y_HI = 2
X = 4
Y_LO = 2
CORES = 2
BLOCKS = Z * Y_HI


def along_z(block, step):
    pairs = [
        (z * Y_HI + y, ((z + step) % Z) * Y_HI + y) for z in range(Z) for y in range(Y_HI)
    ]
    return lax.ppermute(block, "query", pairs)


def across_y(block):
    pairs = [(z * Y_HI + y, z * Y_HI + 1 - y) for z in range(Z) for y in range(Y_HI)]
    return lax.ppermute(block, "query", pairs)


def across_cores(block):
    pairs = [(i, i ^ 1) for i in range(Y_LO * X * CORES)]
    return lax.ppermute(block, "layer", pairs)


def gather_steps(own):
    same, other = {0: own}, {}
    same[-1], same[1], other[0] = along_z(own, 1), along_z(own, -1), across_y(own)
    yield [(0, 0, own), (0, -1, same[-1]), (0, 1, same[1]), (1, 0, other[0])]
    same[-2], same[2] = along_z(same[-1], 1), along_z(same[1], -1)
    other[-1] = across_y(same[-1])
    yield [(0, -2, same[-2]), (0, 2, same[2]), (1, -1, other[-1])]
    same[-3], same[3] = along_z(same[-2], 1), along_z(same[2], -1)
    other[1] = across_y(same[1])
    yield [(0, -3, same[-3]), (0, 3, same[3]), (1, 1, other[1])]
    same[4], other[2] = along_z(same[-3], 1), along_z(other[1], -1)
    other[-2] = across_y(same[-2])
    yield [(0, 4, same[4]), (1, 2, other[2]), (1, -2, other[-2])]
    other[-3], other[3] = along_z(other[-2], 1), along_z(other[2], -1)
    other[4] = across_y(same[4])
    yield [(1, -3, other[-3]), (1, 3, other[3]), (1, 4, other[4])]


def per_device(queries, train_grads, basis_out, basis_in, eig_values, train_order):
    query_rows, local_layers, feat_size = queries.shape
    train_rows = train_grads.shape[0]
    side = basis_out.shape[1]
    grads_full = train_grads.astype(jnp.float32).reshape(train_rows, local_layers, side, side)
    rotated = jnp.einsum(
        "lab,elac,lcd->elbd", basis_out, grads_full, basis_in, precision=lax.Precision.HIGHEST
    )
    scaled = (rotated.reshape(train_rows, local_layers, feat_size) / eig_values[None]).astype(
        jnp.bfloat16
    )
    scaled_flat = scaled.reshape(train_rows, local_layers * feat_size)
    query_flat = queries.reshape(query_rows, local_layers * feat_size)
    layer_devices = lax.axis_size("layer")
    factor = 1.0 / jnp.sqrt(jnp.float32(local_layers * layer_devices * feat_size))

    layer = lax.axis_index("layer")
    query = lax.axis_index("query")
    core = layer % CORES
    own_z, own_y = query // Y_HI, query % Y_HI

    arrived, products = [], []
    for step in gather_steps(scaled_flat):
        arrived += [(column, offset % Z) for column, offset, _ in step]
        rows = jnp.concatenate([block for _, _, block in step], axis=0)
        products.append(
            lax.dot_general(
                rows, query_flat, (((1,), (1,)), ((), ())), preferred_element_type=jnp.float32
            ).astype(jnp.bfloat16)
        )
    partial_sum = jnp.concatenate(products, axis=0)

    block_of = train_order // train_rows
    relative = ((block_of % Y_HI) ^ own_y) * Z + (block_of // Y_HI - own_z) % Z
    place = jnp.zeros_like(relative)
    for at, (column, offset) in enumerate(arrived):
        place = jnp.where(relative == column * Z + offset, at, place)
    place = place * train_rows + train_order % train_rows
    place = place.reshape(Y_LO * X, CORES, train_rows)

    def ordered(for_core):
        rows = lax.dynamic_index_in_dim(place, for_core, 1, keepdims=False).reshape(-1)
        pick = rows[:, None] == jnp.arange(BLOCKS * train_rows)[None, :]
        return lax.dot_general(
            pick.astype(jnp.bfloat16),
            partial_sum,
            (((1,), (0,)), ((), ())),
            preferred_element_type=jnp.float32,
        )

    received = across_cores(ordered(1 - core).astype(jnp.bfloat16))
    chip_sum = (ordered(core) + received.astype(jnp.float32)).astype(jnp.bfloat16)
    groups = [[chip * CORES + c for chip in range(Y_LO * X)] for c in range(CORES)]
    pieces = lax.all_to_all(
        chip_sum.reshape(Y_LO * X, train_rows, query_rows),
        "layer",
        0,
        0,
        axis_index_groups=groups,
        tiled=True,
    )
    return jnp.sum(pieces.astype(jnp.float32), axis=0) * factor


def solution(mesh):
    placed = (
        P("query", "layer", None),
        P("query", "layer", None),
        P("layer", None, None),
        P("layer", None, None),
        P("layer", None),
        P(),
    )
    return jax.shard_map(
        per_device, mesh=mesh, in_specs=placed, out_specs=P("layer", "query"), check_vma=False
    )
```

```python
import jax
import jax.numpy as jnp
from jax import lax
from jax.sharding import PartitionSpec as P

Z = 8
Y_HI = 2
X = 4
Y_LO = 2
CORES = 2
BLOCKS = Z * Y_HI


def along_z(block, step):
    pairs = [
        (z * Y_HI + y, ((z + step) % Z) * Y_HI + y) for z in range(Z) for y in range(Y_HI)
    ]
    return lax.ppermute(block, "query", pairs)


def across_y(block):
    pairs = [(z * Y_HI + y, z * Y_HI + 1 - y) for z in range(Z) for y in range(Y_HI)]
    return lax.ppermute(block, "query", pairs)


def across_cores(block):
    pairs = [(i, i ^ 1) for i in range(Y_LO * X * CORES)]
    return lax.ppermute(block, "layer", pairs)


def together(*arrays):
    return lax.optimization_barrier(arrays)


def gather_steps(own):
    same, other = {0: own}, {}
    same[-1], same[1], other[0] = along_z(own, 1), along_z(own, -1), across_y(own)

    same[-1], same[1] = together(same[-1], same[1])
    same[-2], same[2] = along_z(same[-1], 1), along_z(same[1], -1)
    other[-1] = across_y(same[-1])

    same[-2], same[2], next_y, other[0] = together(same[-2], same[2], same[1], other[0])
    same[-3], same[3] = along_z(same[-2], 1), along_z(same[2], -1)
    other[1] = across_y(next_y)

    same[-3], same[3], other[-1] = together(same[-3], same[3], other[-1])
    other[-2], same[4] = along_z(other[-1], 1), along_z(same[3], -1)
    other[3] = across_y(same[3])

    other[-2], same[4], other[1] = together(other[-2], same[4], other[1])
    other[-3], other[2] = along_z(other[-2], 1), along_z(other[1], -1)
    other[4] = across_y(same[4])

    yield [(0, 0, own), (0, -1, same[-1]), (0, 1, same[1]), (1, 0, other[0])]
    yield [(0, -2, same[-2]), (0, 2, same[2]), (1, -1, other[-1])]
    yield [(0, -3, same[-3]), (0, 3, same[3]), (1, 1, other[1])]
    yield [(1, -2, other[-2]), (0, 4, same[4]), (1, 3, other[3])]
    yield [(1, -3, other[-3]), (1, 2, other[2]), (1, 4, other[4])]


def per_device(queries, train_grads, basis_out, basis_in, eig_values, train_order):
    query_rows, local_layers, feat_size = queries.shape
    train_rows = train_grads.shape[0]
    side = basis_out.shape[1]
    grads_full = train_grads.astype(jnp.float32).reshape(train_rows, local_layers, side, side)
    rotated = jnp.einsum(
        "lab,elac,lcd->elbd", basis_out, grads_full, basis_in, precision=lax.Precision.HIGHEST
    )
    scaled = (rotated.reshape(train_rows, local_layers, feat_size) / eig_values[None]).astype(
        jnp.bfloat16
    )
    scaled_flat = scaled.reshape(train_rows, local_layers * feat_size)
    query_flat = queries.reshape(query_rows, local_layers * feat_size)
    layer_devices = lax.axis_size("layer")
    factor = 1.0 / jnp.sqrt(jnp.float32(local_layers * layer_devices * feat_size))

    layer = lax.axis_index("layer")
    query = lax.axis_index("query")
    core = layer % CORES
    own_z, own_y = query // Y_HI, query % Y_HI

    arrived, products = [], []
    for step in gather_steps(scaled_flat):
        arrived += [(column, offset % Z) for column, offset, _ in step]
        rows = jnp.concatenate([block for _, _, block in step], axis=0)
        products.append(
            lax.dot_general(
                rows, query_flat, (((1,), (1,)), ((), ())), preferred_element_type=jnp.float32
            ).astype(jnp.bfloat16)
        )
    block_of = train_order // train_rows
    relative = ((block_of % Y_HI) ^ own_y) * Z + (block_of // Y_HI - own_z) % Z
    place = jnp.zeros_like(relative)
    for at, (column, offset) in enumerate(arrived):
        place = jnp.where(relative == column * Z + offset, at, place)
    place = place * train_rows + train_order % train_rows
    place = place.reshape(Y_LO * X, CORES, train_rows)

    early = jnp.concatenate(products[:-1], axis=0)
    early_rows = early.shape[0]

    def pick(rows, first, count):
        return (rows[:, None] == first + jnp.arange(count)[None, :]).astype(jnp.bfloat16)

    def times(chosen, values):
        return lax.dot_general(
            chosen, values, (((1,), (0,)), ((), ())), preferred_element_type=jnp.float32
        )

    def ordered(for_core):
        rows = lax.dynamic_index_in_dim(place, for_core, 1, keepdims=False).reshape(-1)
        before = times(pick(rows, 0, early_rows), early).astype(jnp.bfloat16)
        late = pick(rows, early_rows, products[-1].shape[0])
        return before, late

    other_before, other_late = ordered(1 - core)
    own_before, own_late = ordered(core)
    other_half = (other_before + times(other_late, products[-1])).astype(jnp.bfloat16)
    received = across_cores(other_half)
    own_half = (own_before + times(own_late, products[-1])).astype(jnp.bfloat16)
    own_half, received = together(own_half, received)
    chip_sum = (own_half.astype(jnp.float32) + received.astype(jnp.float32)).astype(jnp.bfloat16)
    groups = [[chip * CORES + c for chip in range(Y_LO * X)] for c in range(CORES)]
    pieces = lax.all_to_all(
        chip_sum.reshape(Y_LO * X, train_rows, query_rows),
        "layer",
        0,
        0,
        axis_index_groups=groups,
        tiled=True,
    )
    return jnp.sum(pieces.astype(jnp.float32), axis=0) * factor


def solution(mesh):
    placed = (
        P("query", "layer", None),
        P("query", "layer", None),
        P("layer", None, None),
        P("layer", None, None),
        P("layer", None),
        P(),
    )
    return jax.shard_map(
        per_device, mesh=mesh, in_specs=placed, out_specs=P("layer", "query"), check_vma=False
    )
```

```python
import jax
import jax.numpy as jnp
from jax import lax
from jax.sharding import PartitionSpec as P

Z = 8
Y_HI = 2
X = 4
Y_LO = 2
CORES = 2


def along_z(block, step):
    pairs = [
        (z * Y_HI + y, ((z + step) % Z) * Y_HI + y) for z in range(Z) for y in range(Y_HI)
    ]
    return lax.ppermute(block, "query", pairs)


def across_y(block):
    pairs = [(z * Y_HI + y, z * Y_HI + 1 - y) for z in range(Z) for y in range(Y_HI)]
    return lax.ppermute(block, "query", pairs)


def across_cores(block):
    pairs = [(i, i ^ 1) for i in range(Y_LO * X * CORES)]
    return lax.ppermute(block, "layer", pairs)


def together(*arrays):
    return lax.optimization_barrier(arrays)


def gather_steps(own):
    half = own.shape[0] // 2

    def upper(block):
        return block[:half]

    def lower(block):
        return block[half:]

    def join(first, second):
        return jnp.concatenate([first, second], axis=0)

    def whole(column, offset):
        return [(column, offset, 0), (column, offset, 1)]

    back1, front1, across0 = along_z(own, 1), along_z(own, -1), across_y(own)

    back1, front1 = together(back1, front1)
    back2, front2 = along_z(back1, 1), along_z(front1, -1)
    across1 = across_y(join(upper(back1), lower(front1)))

    back2, front2, across0 = together(back2, front2, across0)
    back3, front3 = along_z(back2, 1), along_z(front2, -1)
    across2 = across_y(join(upper(front2), lower(back2)))

    back3, front3, across1 = together(back3, front3, across1)
    back4 = along_z(join(upper(back3), upper(across1)), 1)
    front4 = along_z(join(lower(front3), lower(across1)), -1)
    across3 = across_y(join(upper(back3), lower(front3)))

    back4, front4, across2 = together(back4, front4, across2)
    back5 = along_z(join(lower(across0), lower(across2)), 1)
    front5 = along_z(join(upper(across0), upper(across2)), -1)
    across4 = across_y(join(upper(back4), upper(front4)))

    yield [own, back1, front1, across0], whole(0, 0) + whole(0, -1) + whole(0, 1) + whole(1, 0)
    yield [back2, front2, across1], whole(0, -2) + whole(0, 2) + [(1, -1, 0), (1, 1, 1)]
    yield [back3, front3, across2], whole(0, -3) + whole(0, 3) + [(1, 2, 0), (1, -2, 1)]
    yield [back4, front4, across3], [
        (0, 4, 0), (1, -2, 0), (0, 4, 1), (1, 2, 1), (1, -3, 0), (1, 3, 1)
    ]
    yield [back5, front5, across4], [
        (1, -1, 1), (1, -3, 1), (1, 1, 0), (1, 3, 0), (1, 4, 0), (1, 4, 1)
    ]


def per_device(queries, train_grads, basis_out, basis_in, eig_values, train_order):
    query_rows, local_layers, feat_size = queries.shape
    train_rows = train_grads.shape[0]
    side = basis_out.shape[1]
    grads_full = train_grads.astype(jnp.float32).reshape(train_rows, local_layers, side, side)
    rotated = jnp.einsum(
        "lab,elac,lcd->elbd", basis_out, grads_full, basis_in, precision=lax.Precision.HIGH
    )
    scaled = (rotated.reshape(train_rows, local_layers, feat_size) / eig_values[None]).astype(
        jnp.bfloat16
    )
    scaled_flat = scaled.reshape(train_rows, local_layers * feat_size)
    query_flat = queries.reshape(query_rows, local_layers * feat_size)
    layer_devices = lax.axis_size("layer")
    factor = 1.0 / jnp.sqrt(jnp.float32(local_layers * layer_devices * feat_size))

    layer = lax.axis_index("layer")
    query = lax.axis_index("query")
    core = layer % CORES
    own_z, own_y = query // Y_HI, query % Y_HI

    arrived, products = [], []
    for blocks, names in gather_steps(scaled_flat):
        arrived += names
        rows = jnp.concatenate(blocks, axis=0)
        products.append(
            lax.dot_general(
                rows, query_flat, (((1,), (1,)), ((), ())), preferred_element_type=jnp.float32
            ).astype(jnp.bfloat16)
        )

    half_rows = train_rows // 2
    half_of = train_order // half_rows
    block_of = half_of // 2
    relative = ((block_of % Y_HI) ^ own_y) * Z + (block_of // Y_HI - own_z) % Z
    relative = relative * 2 + half_of % 2
    place = jnp.zeros_like(relative)
    for at, (column, offset, part) in enumerate(arrived):
        place = jnp.where(relative == (column * Z + offset % Z) * 2 + part, at, place)
    place = place * half_rows + train_order % half_rows
    place = place.reshape(Y_LO * X, CORES, train_rows)

    early = jnp.concatenate(products[:-1], axis=0)
    early_rows = early.shape[0]

    def pick(rows, first, count):
        return (rows[:, None] == first + jnp.arange(count)[None, :]).astype(jnp.bfloat16)

    def times(chosen, values):
        return lax.dot_general(
            chosen, values, (((1,), (0,)), ((), ())), preferred_element_type=jnp.float32
        )

    def ordered(for_core):
        rows = lax.dynamic_index_in_dim(place, for_core, 1, keepdims=False).reshape(-1)
        before = times(pick(rows, 0, early_rows), early).astype(jnp.bfloat16)
        late = pick(rows, early_rows, products[-1].shape[0])
        return before, late

    other_before, other_late = ordered(1 - core)
    own_before, own_late = ordered(core)
    other_half = (other_before + times(other_late, products[-1])).astype(jnp.bfloat16)
    received = across_cores(other_half)
    own_half = (own_before + times(own_late, products[-1])).astype(jnp.bfloat16)
    own_half, received = together(own_half, received)
    chip_sum = own_half.astype(jnp.float32) + received.astype(jnp.float32)
    chip_sum = (chip_sum * factor).astype(jnp.bfloat16)
    groups = [[chip * CORES + c for chip in range(Y_LO * X)] for c in range(CORES)]
    pieces = lax.all_to_all(
        chip_sum.reshape(Y_LO * X, train_rows, query_rows),
        "layer",
        0,
        0,
        axis_index_groups=groups,
        tiled=True,
    )
    return jnp.sum(pieces.astype(jnp.float32), axis=0)


def solution(mesh):
    placed = (
        P("query", "layer", None),
        P("query", "layer", None),
        P("layer", None, None),
        P("layer", None, None),
        P("layer", None),
        P(),
    )
    return jax.shard_map(
        per_device, mesh=mesh, in_specs=placed, out_specs=P("layer", "query"), check_vma=False
    )
```

```python
import jax
import jax.numpy as jnp
from jax import lax
from jax.sharding import PartitionSpec as P

Z = 8
Y_HI = 2
X = 4
Y_LO = 2
CORES = 2


def along_z(block, step):
    pairs = [
        (z * Y_HI + y, ((z + step) % Z) * Y_HI + y) for z in range(Z) for y in range(Y_HI)
    ]
    return lax.ppermute(block, "query", pairs)


def across_y(block):
    pairs = [(z * Y_HI + y, z * Y_HI + 1 - y) for z in range(Z) for y in range(Y_HI)]
    return lax.ppermute(block, "query", pairs)


def across_cores(block):
    pairs = [(i, i ^ 1) for i in range(Y_LO * X * CORES)]
    return lax.ppermute(block, "layer", pairs)


def together(*arrays):
    return lax.optimization_barrier(arrays)


def gather_steps(own):
    half = own.shape[0] // 2

    def upper(block):
        return block[:half]

    def lower(block):
        return block[half:]

    def join(first, second):
        return jnp.concatenate([first, second], axis=0)

    def whole(column, offset):
        return [(column, offset, 0), (column, offset, 1)]

    back1, front1, across0 = along_z(own, 1), along_z(own, -1), across_y(own)

    back1, front1 = together(back1, front1)
    back2, front2 = along_z(back1, 1), along_z(front1, -1)
    across1 = across_y(join(upper(back1), lower(front1)))

    back2, front2, across0 = together(back2, front2, across0)
    back3, front3 = along_z(back2, 1), along_z(front2, -1)
    across2 = across_y(join(upper(front2), lower(back2)))

    back3, front3, across1 = together(back3, front3, across1)
    to_front, to_back = together(
        join(upper(back3), upper(across1)), join(lower(front3), lower(across1))
    )
    back4, front4 = along_z(to_front, 1), along_z(to_back, -1)
    across3 = across_y(join(upper(to_front), upper(to_back)))

    to_front, to_back = together(
        join(lower(across0), lower(across2)), join(upper(across0), upper(across2))
    )
    back4, front4, to_front, to_back = together(back4, front4, to_front, to_back)
    back5, front5 = along_z(to_front, 1), along_z(to_back, -1)
    to_across, _, _ = together(join(upper(back4), upper(front4)), to_front, to_back)
    across4 = across_y(to_across)

    yield [own, back1, front1, across0], whole(0, 0) + whole(0, -1) + whole(0, 1) + whole(1, 0)
    yield [back2, front2, across1], whole(0, -2) + whole(0, 2) + [(1, -1, 0), (1, 1, 1)]
    yield [back3, front3, across2], whole(0, -3) + whole(0, 3) + [(1, 2, 0), (1, -2, 1)]
    yield [back4, front4, across3], [
        (0, 4, 0), (1, -2, 0), (0, 4, 1), (1, 2, 1), (1, -3, 0), (1, 3, 1)
    ]
    yield [back5, front5, across4], [
        (1, -1, 1), (1, -3, 1), (1, 1, 0), (1, 3, 0), (1, 4, 0), (1, 4, 1)
    ]


def per_device(queries, train_grads, basis_out, basis_in, eig_values, train_order):
    query_rows, local_layers, feat_size = queries.shape
    train_rows = train_grads.shape[0]
    side = basis_out.shape[1]
    grads_full = train_grads.astype(jnp.float32).reshape(train_rows, local_layers, side, side)
    rotated = jnp.einsum(
        "lab,elac,lcd->elbd", basis_out, grads_full, basis_in, precision=lax.Precision.HIGH
    )
    scaled = (rotated.reshape(train_rows, local_layers, feat_size) / eig_values[None]).astype(
        jnp.bfloat16
    )
    scaled_flat = scaled.reshape(train_rows, local_layers * feat_size)
    query_flat = queries.reshape(query_rows, local_layers * feat_size)
    layer_devices = lax.axis_size("layer")
    factor = 1.0 / jnp.sqrt(jnp.float32(local_layers * layer_devices * feat_size))

    layer = lax.axis_index("layer")
    query = lax.axis_index("query")
    core = layer % CORES
    own_z, own_y = query // Y_HI, query % Y_HI

    def times_queries(blocks):
        return lax.dot_general(
            jnp.concatenate(blocks, axis=0),
            query_flat,
            (((1,), (1,)), ((), ())),
            preferred_element_type=jnp.float32,
        ).astype(jnp.bfloat16)

    *steps, (last_blocks, last_names) = gather_steps(scaled_flat)
    arrived = [name for _, names in steps for name in names] + last_names
    products = [times_queries(blocks) for blocks, _ in steps]

    half_rows = train_rows // 2
    half_of = train_order // half_rows
    block_of = half_of // 2
    relative = ((block_of % Y_HI) ^ own_y) * Z + (block_of // Y_HI - own_z) % Z
    relative = relative * 2 + half_of % 2
    place = jnp.zeros_like(relative)
    for at, (column, offset, part) in enumerate(arrived):
        place = jnp.where(relative == (column * Z + offset % Z) * 2 + part, at, place)
    place = place * half_rows + train_order % half_rows
    place = place.reshape(Y_LO * X, CORES, train_rows)

    early = jnp.concatenate(products, axis=0)
    early_rows = early.shape[0]

    def pick(rows, first, count):
        return (rows[:, None] == first + jnp.arange(count)[None, :]).astype(jnp.bfloat16)

    def times(chosen, values):
        return lax.dot_general(
            chosen, values, (((1,), (0,)), ((), ())), preferred_element_type=jnp.float32
        )

    def rows_of(for_core):
        return lax.dynamic_index_in_dim(place, for_core, 1, keepdims=False).reshape(-1)

    own_rows, other_rows = rows_of(core), rows_of(1 - core)
    own_before = times(pick(own_rows, 0, early_rows), early).astype(jnp.bfloat16)
    other_before = times(pick(other_rows, 0, early_rows), early).astype(jnp.bfloat16)
    *last_blocks, own_before, other_before = together(*last_blocks, own_before, other_before)
    late = times_queries(last_blocks)

    def with_late(before, rows):
        chosen = pick(rows, early_rows, late.shape[0])
        return (before + times(chosen, late)).astype(jnp.bfloat16)

    other_half = with_late(other_before, other_rows)
    received = across_cores(other_half)
    own_half = with_late(own_before, own_rows)
    own_half, received = together(own_half, received)
    chip_sum = own_half.astype(jnp.float32) + received.astype(jnp.float32)
    chip_sum = (chip_sum * factor).astype(jnp.bfloat16)
    groups = [[chip * CORES + c for chip in range(Y_LO * X)] for c in range(CORES)]
    pieces = lax.all_to_all(
        chip_sum.reshape(Y_LO * X, train_rows, query_rows),
        "layer",
        0,
        0,
        axis_index_groups=groups,
        tiled=True,
    )
    return jnp.sum(pieces.astype(jnp.float32), axis=0)


def solution(mesh):
    placed = (
        P("query", "layer", None),
        P("query", "layer", None),
        P("layer", None, None),
        P("layer", None, None),
        P("layer", None),
        P(),
    )
    return jax.shard_map(
        per_device, mesh=mesh, in_specs=placed, out_specs=P("layer", "query"), check_vma=False
    )
```

```python
import jax
import jax.numpy as jnp
from jax import lax
from jax.sharding import PartitionSpec as P

Z = 8
Y_HI = 2
X = 4
Y_LO = 2
CORES = 2


def along_z(block, step):
    pairs = [
        (z * Y_HI + y, ((z + step) % Z) * Y_HI + y) for z in range(Z) for y in range(Y_HI)
    ]
    return lax.ppermute(block, "query", pairs)


def across_y(block):
    pairs = [(z * Y_HI + y, z * Y_HI + 1 - y) for z in range(Z) for y in range(Y_HI)]
    return lax.ppermute(block, "query", pairs)


def across_cores(block):
    pairs = [(i, i ^ 1) for i in range(Y_LO * X * CORES)]
    return lax.ppermute(block, "layer", pairs)


def together(*arrays):
    return lax.optimization_barrier(arrays)


def gather_steps(own):
    half = own.shape[0] // 2

    def upper(block):
        return block[:half]

    def lower(block):
        return block[half:]

    def join(first, second):
        return jnp.concatenate([first, second], axis=0)

    def whole(column, offset):
        return [(column, offset, 0), (column, offset, 1)]

    back1, front1, across0 = along_z(own, 1), along_z(own, -1), across_y(own)

    back1, front1 = together(back1, front1)
    back2, front2 = along_z(back1, 1), along_z(front1, -1)
    across1 = across_y(join(upper(back1), lower(front1)))

    back2, front2, across0 = together(back2, front2, across0)
    back3, front3 = along_z(back2, 1), along_z(front2, -1)
    across2 = across_y(join(upper(front2), lower(back2)))

    back3, front3, across1 = together(back3, front3, across1)
    to_front, to_back = together(
        join(upper(back3), upper(across1)), join(lower(front3), lower(across1))
    )
    back4, front4 = along_z(to_front, 1), along_z(to_back, -1)
    across3 = across_y(join(upper(to_front), upper(to_back)))

    to_front, to_back = together(
        join(lower(across0), lower(across2)), join(upper(across0), upper(across2))
    )
    back4, front4, to_front, to_back = together(back4, front4, to_front, to_back)
    back5, front5 = along_z(to_front, 1), along_z(to_back, -1)
    to_across, _, _ = together(join(upper(back4), upper(front4)), to_front, to_back)
    across4 = across_y(to_across)

    yield [own, back1, front1, across0], whole(0, 0) + whole(0, -1) + whole(0, 1) + whole(1, 0)
    yield [back2, front2, across1], whole(0, -2) + whole(0, 2) + [(1, -1, 0), (1, 1, 1)]
    yield [back3, front3, across2], whole(0, -3) + whole(0, 3) + [(1, 2, 0), (1, -2, 1)]
    yield [back4, front4, across3], [
        (0, 4, 0), (1, -2, 0), (0, 4, 1), (1, 2, 1), (1, -3, 0), (1, 3, 1)
    ]
    yield [back5, front5, across4], [
        (1, -1, 1), (1, -3, 1), (1, 1, 0), (1, 3, 0), (1, 4, 0), (1, 4, 1)
    ]


def per_device(queries, train_grads, basis_out, basis_in, eig_values, train_order):
    query_rows, local_layers, feat_size = queries.shape
    train_rows = train_grads.shape[0]
    side = basis_out.shape[1]
    grads_full = train_grads.astype(jnp.float32).reshape(train_rows, local_layers, side, side)
    rotated = jnp.einsum(
        "lab,elac,lcd->elbd", basis_out, grads_full, basis_in, precision=lax.Precision.HIGH
    )
    scaled = (rotated.reshape(train_rows, local_layers, feat_size) / eig_values[None]).astype(
        jnp.bfloat16
    )
    scaled_flat = scaled.reshape(train_rows, local_layers * feat_size)
    query_flat = queries.reshape(query_rows, local_layers * feat_size)
    layer_devices = lax.axis_size("layer")
    factor = 1.0 / jnp.sqrt(jnp.float32(local_layers * layer_devices * feat_size))

    layer = lax.axis_index("layer")
    query = lax.axis_index("query")
    core = layer % CORES
    own_z, own_y = query // Y_HI, query % Y_HI

    def times_queries(blocks):
        return lax.dot_general(
            jnp.concatenate(blocks, axis=0),
            query_flat,
            (((1,), (1,)), ((), ())),
            preferred_element_type=jnp.float32,
        ).astype(jnp.bfloat16)

    *steps, (last_blocks, last_names) = gather_steps(scaled_flat)
    arrived = [name for _, names in steps for name in names] + last_names
    products = [times_queries(blocks) for blocks, _ in steps]

    half_rows = train_rows // 2
    half_of = train_order // half_rows
    block_of = half_of // 2
    relative = ((block_of % Y_HI) ^ own_y) * Z + (block_of // Y_HI - own_z) % Z
    relative = relative * 2 + half_of % 2
    place = jnp.zeros_like(relative)
    for at, (column, offset, part) in enumerate(arrived):
        place = jnp.where(relative == (column * Z + offset % Z) * 2 + part, at, place)
    place = place * half_rows + train_order % half_rows
    place = place.reshape(Y_LO * X, CORES, train_rows)

    early = jnp.concatenate(products, axis=0)
    early_rows = early.shape[0]

    def pick(rows, first, count):
        return (rows[:, None] == first + jnp.arange(count)[None, :]).astype(jnp.bfloat16)

    def times(chosen, values):
        return lax.dot_general(
            chosen, values, (((1,), (0,)), ((), ())), preferred_element_type=jnp.float32
        )

    def rows_of(for_core):
        return lax.dynamic_index_in_dim(place, for_core, 1, keepdims=False).reshape(-1)

    own_rows, other_rows = rows_of(core), rows_of(1 - core)
    own_before = times(pick(own_rows, 0, early_rows), early).astype(jnp.bfloat16)
    other_before = times(pick(other_rows, 0, early_rows), early).astype(jnp.bfloat16)
    received = across_cores(other_before)
    *last_blocks, own_before = together(*last_blocks, own_before)
    late = times_queries(last_blocks)
    early_sum = own_before.astype(jnp.float32) + received.astype(jnp.float32)
    early_sum = (early_sum * factor).astype(jnp.bfloat16)
    late_sum = late.astype(jnp.float32) + across_cores(late).astype(jnp.float32)
    late_sum = (late_sum * factor).astype(jnp.bfloat16)
    chip_sum = early_sum + times(pick(own_rows, early_rows, late.shape[0]), late_sum)
    chip_sum = chip_sum.astype(jnp.bfloat16)
    groups = [[chip * CORES + c for chip in range(Y_LO * X)] for c in range(CORES)]
    pieces = lax.all_to_all(
        chip_sum.reshape(Y_LO * X, train_rows, query_rows),
        "layer",
        0,
        0,
        axis_index_groups=groups,
        tiled=True,
    )
    return jnp.sum(pieces.astype(jnp.float32), axis=0)


def solution(mesh):
    placed = (
        P("query", "layer", None),
        P("query", "layer", None),
        P("layer", None, None),
        P("layer", None, None),
        P("layer", None),
        P(),
    )
    return jax.shard_map(
        per_device, mesh=mesh, in_specs=placed, out_specs=P("layer", "query"), check_vma=False
    )
```

```python
import jax
import jax.numpy as jnp
from jax import lax
from jax.sharding import PartitionSpec as P

Z = 8
Y_HI = 2
X = 4
Y_LO = 2
CORES = 2


def along_z(block, step):
    pairs = [
        (z * Y_HI + y, ((z + step) % Z) * Y_HI + y) for z in range(Z) for y in range(Y_HI)
    ]
    return lax.ppermute(block, "query", pairs)


def across_y(block):
    pairs = [(z * Y_HI + y, z * Y_HI + 1 - y) for z in range(Z) for y in range(Y_HI)]
    return lax.ppermute(block, "query", pairs)


def across_cores(block):
    pairs = [(i, i ^ 1) for i in range(Y_LO * X * CORES)]
    return lax.ppermute(block, "layer", pairs)


def together(*arrays):
    return lax.optimization_barrier(arrays)


def gather_steps(own):
    half = own.shape[0] // 2

    def upper(block):
        return block[:half]

    def lower(block):
        return block[half:]

    def join(first, second):
        return jnp.concatenate([first, second], axis=0)

    def whole(column, offset):
        return [(column, offset, 0), (column, offset, 1)]

    back1, front1, across0 = along_z(own, 1), along_z(own, -1), across_y(own)

    back1, front1 = together(back1, front1)
    back2, front2 = along_z(back1, 1), along_z(front1, -1)
    across1 = across_y(join(upper(back1), lower(front1)))

    back2, front2, across0 = together(back2, front2, across0)
    back3, front3 = along_z(back2, 1), along_z(front2, -1)
    across2 = across_y(join(upper(front2), lower(back2)))

    back3, front3, across1 = together(back3, front3, across1)
    to_front, to_back = together(
        join(upper(back3), upper(across1)), join(lower(front3), lower(across1))
    )
    back4, front4 = along_z(to_front, 1), along_z(to_back, -1)
    across3 = across_y(join(upper(to_front), upper(to_back)))

    to_front, to_back = together(
        join(lower(across0), lower(across2)), join(upper(across0), upper(across2))
    )
    back4, front4, to_front, to_back = together(back4, front4, to_front, to_back)
    back5, front5 = along_z(to_front, 1), along_z(to_back, -1)
    across4 = across_y(join(upper(back4), upper(front4)))

    yield [own, back1, front1, across0], whole(0, 0) + whole(0, -1) + whole(0, 1) + whole(1, 0)
    yield [back2, front2, across1], whole(0, -2) + whole(0, 2) + [(1, -1, 0), (1, 1, 1)]
    yield [back3, front3, across2], whole(0, -3) + whole(0, 3) + [(1, 2, 0), (1, -2, 1)]
    yield [back4, front4, across3], [
        (0, 4, 0), (1, -2, 0), (0, 4, 1), (1, 2, 1), (1, -3, 0), (1, 3, 1)
    ]
    yield [back5, front5, across4], [
        (1, -1, 1), (1, -3, 1), (1, 1, 0), (1, 3, 0), (1, 4, 0), (1, 4, 1)
    ]


def per_device(queries, train_grads, basis_out, basis_in, eig_values, train_order):
    query_rows, local_layers, feat_size = queries.shape
    train_rows = train_grads.shape[0]
    side = basis_out.shape[1]
    grads_full = train_grads.astype(jnp.float32).reshape(train_rows, local_layers, side, side)
    rotated = jnp.einsum(
        "lab,elac,lcd->elbd", basis_out, grads_full, basis_in, precision=lax.Precision.HIGH
    )
    scaled = (rotated.reshape(train_rows, local_layers, feat_size) / eig_values[None]).astype(
        jnp.bfloat16
    )
    scaled_flat = scaled.reshape(train_rows, local_layers * feat_size)
    query_flat = queries.reshape(query_rows, local_layers * feat_size)
    layer_devices = lax.axis_size("layer")
    factor = 1.0 / jnp.sqrt(jnp.float32(local_layers * layer_devices * feat_size))

    layer = lax.axis_index("layer")
    query = lax.axis_index("query")
    core = layer % CORES
    own_z, own_y = query // Y_HI, query % Y_HI

    def times_queries(blocks):
        return lax.dot_general(
            jnp.concatenate(blocks, axis=0),
            query_flat,
            (((1,), (1,)), ((), ())),
            preferred_element_type=jnp.float32,
        ).astype(jnp.bfloat16)

    *steps, (last_blocks, last_names) = gather_steps(scaled_flat)
    arrived = [name for _, names in steps for name in names] + last_names
    products = [times_queries(blocks) for blocks, _ in steps]

    half_rows = train_rows // 2
    half_of = train_order // half_rows
    block_of = half_of // 2
    relative = ((block_of % Y_HI) ^ own_y) * Z + (block_of // Y_HI - own_z) % Z
    relative = relative * 2 + half_of % 2
    place = jnp.zeros_like(relative)
    for at, (column, offset, part) in enumerate(arrived):
        place = jnp.where(relative == (column * Z + offset % Z) * 2 + part, at, place)
    place = place * half_rows + train_order % half_rows
    place = place.reshape(Y_LO * X, CORES, train_rows)

    early = jnp.concatenate(products, axis=0)
    early_rows = early.shape[0]

    def pick(rows, first, count):
        return (rows[:, None] == first + jnp.arange(count)[None, :]).astype(jnp.bfloat16)

    def times(chosen, values):
        return lax.dot_general(
            chosen, values, (((1,), (0,)), ((), ())), preferred_element_type=jnp.float32
        )

    def rows_of(for_core):
        return lax.dynamic_index_in_dim(place, for_core, 1, keepdims=False).reshape(-1)

    own_rows, other_rows = rows_of(core), rows_of(1 - core)
    own_before = times(pick(own_rows, 0, early_rows), early).astype(jnp.bfloat16)
    other_before = times(pick(other_rows, 0, early_rows), early).astype(jnp.bfloat16)
    received = across_cores(other_before)
    *last_blocks, own_before = together(*last_blocks, own_before)
    late = times_queries(last_blocks)
    early_sum = own_before.astype(jnp.float32) + received.astype(jnp.float32)
    early_sum = (early_sum * factor).astype(jnp.bfloat16)
    late_sum = late.astype(jnp.float32) + across_cores(late).astype(jnp.float32)
    late_sum = (late_sum * factor).astype(jnp.bfloat16)
    chip_sum = early_sum + times(pick(own_rows, early_rows, late.shape[0]), late_sum)
    chip_sum = chip_sum.astype(jnp.bfloat16)
    groups = [[chip * CORES + c for chip in range(Y_LO * X)] for c in range(CORES)]
    pieces = lax.all_to_all(
        chip_sum.reshape(Y_LO * X, train_rows, query_rows),
        "layer",
        0,
        0,
        axis_index_groups=groups,
        tiled=True,
    )
    return jnp.sum(pieces.astype(jnp.float32), axis=0)


def solution(mesh):
    placed = (
        P("query", "layer", None),
        P("query", "layer", None),
        P("layer", None, None),
        P("layer", None, None),
        P("layer", None),
        P(),
    )
    return jax.shard_map(
        per_device, mesh=mesh, in_specs=placed, out_specs=P("layer", "query"), check_vma=False
    )
```
